128 devices in a mesh: wide: 16 (over x, z), narrow: 8 (over y, core).
Axes of the slice: x: 4, y: 4, z: 4, core: 2. Of those that a mesh axis runs over, the one named last changes fastest.
Arguments:
- leaf_density: bfloat16 [98304, 152], P(('wide', 'narrow')), may hold values from -6 to 6
- m2l_matrices: bfloat16 [189, 152, 152], replicated, may hold values from -0.03125 to 0.03125
- m2m_matrices: bfloat16 [8, 152, 152], replicated, may hold values from -0.15625 to 0.15625
- send_index: int32 [128, 128, 128], P(('wide', 'narrow')), may hold values from 0 to 767
- leaf_source: int32 [189, 98304], P(None, ('wide', 'narrow')), may hold values from -1 to 17151, as said below
- coarse_source: int32 [189, 12288], P(None, ('wide', 'narrow')), may hold values from -1 to 12287, as said below
Outputs:
- leaf_local: float32 [98304, 152], P(('wide', 'narrow'))
- coarse_multipole: bfloat16 [12288, 152], P(('wide', 'narrow'))
- coarse_local: float32 [12288, 152], P(('wide', 'narrow'))
The draws below stay inside these ranges and needn't reach their ends.
Inputs may be any that keep to these rules, and one draw needn't show every extreme that they name: `leaf_source`: -1 marks an absent source. 0 to 767 is a cell of the target's own device. A larger value 768 + p * 128 + k names slot k of what device p sends to the target's device, where p is another device; for each such pair only a leading run of slots is named, and for every device all 128 slots of some one pair are. `coarse_source`: -1 marks an absent source. Otherwise the source lies in the target's own index of wide or in the one beside it, counting 8 * 96 parent cells to an index of wide.
All inputs are finite; a program needn't handle non-finite values.
Results may differ from the reference program's by a relative error of at most 0.0029.
Values may be sent and summed in bfloat16 or wider, within the bound.
No kernel may reach another device: no remote copies, remote signals or barrier semaphores. Data moves between devices by JAX's collectives and lax.ppermute only.
A program may use at most 128 MiB of HBM per device.

```python
import jax
import jax.numpy as jnp
from jax import lax

P_SIZE = 152
NOFF = 189
C = 768
CAP = 128
CELLS = 98304
NPAR = 12288
N_WIDE = 16
N_NARROW = 8
DEVICES = 128


def draw_leaf_source(key, part):
    key = jax.random.fold_in(key, 11)
    keys = jax.random.split(key, 6)
    devices_all = jnp.arange(DEVICES, dtype=jnp.int32)
    counts = jax.random.randint(keys[0], (DEVICES, DEVICES), CAP // 2, CAP + 1)
    full = (devices_all + 1 + jax.random.randint(keys[1], (DEVICES,), 0, DEVICES - 1)) % DEVICES
    full = jnp.where(devices_all == 0, DEVICES - 1, full).astype(jnp.int32)
    counts = jnp.where(devices_all[None, :] == full[:, None], CAP, counts)
    shape = (NOFF, CELLS)
    cell = jnp.broadcast_to(jnp.arange(CELLS, dtype=jnp.int32)[None, :], shape)
    device = cell // C
    offset = jnp.broadcast_to(jnp.arange(NOFF, dtype=jnp.int32)[:, None], shape)
    kind = jax.random.randint(keys[2], shape, 0, 10)
    local = jax.random.randint(keys[3], shape, 0, C)
    step = jax.random.randint(keys[4], shape, 1, DEVICES)
    peer = (device + step) % DEVICES
    live = counts[device, peer]
    slot = jax.random.randint(keys[5], shape, 0, 1 << 20) % live
    forced = jnp.logical_and(cell % C == 0, offset < CAP)
    peer = jnp.where(forced, full[device], peer)
    slot = jnp.where(forced, offset, slot)
    ghost = C + peer * CAP + slot
    out = jnp.where(forced, ghost, jnp.where(kind < 3, -1, jnp.where(kind < 5, local, ghost)))
    return out.astype(jnp.int32)


def draw_coarse_source(key, part):
    key = jax.random.fold_in(key, 23)
    keys = jax.random.split(key, 2)
    group_rows = N_NARROW * (C // 8)
    shape = (NOFF, NPAR)
    group = jnp.broadcast_to((jnp.arange(NPAR, dtype=jnp.int32) // group_rows)[None, :], shape)
    kind = jax.random.randint(keys[0], shape, 0, 10)
    delta = jnp.where(kind == 7, -1, jnp.where(kind == 8, 1, 0))
    target = jnp.clip(group + delta, 0, N_WIDE - 1)
    inside = jax.random.randint(keys[1], shape, 0, group_rows)
    out = jnp.where(kind < 3, -1, target * group_rows + inside)
    return out.astype(jnp.int32)


def touch_ends(values, own_key, low, top_value):
    place = [jax.random.randint(jax.random.fold_in(own_key, axis), (), 0, length) for axis, length in enumerate(values.shape)]
    widest = values.shape.index(max(values.shape))
    next_to = place[:widest] + [(place[widest] + 1) % values.shape[widest]] + place[widest + 1:]
    return values.at[tuple(place)].set(low).at[tuple(next_to)].set(top_value)


def level_of(rng, dims, pieces, low, high):
    def one(position, parts):
        heights = jax.random.uniform(jax.random.fold_in(jax.random.fold_in(rng, 6), position), (parts,), jnp.float32, low / len(pieces), high / len(pieces))
        return jnp.repeat(jnp.exp(heights), dims[position] // parts).reshape((-1,) + (1,) * (len(dims) - position - 1))

    factor_of = one(*pieces[0])
    for cut in pieces[1:]:
        factor_of = factor_of * one(*cut)
    return factor_of


def scatter_about(stream_key, shape, scale, most, shards=(), kind=jnp.bfloat16):
    result = jax.random.normal(stream_key, shape, jnp.float32) * scale
    if len(shards) > 0:
        result = level_of(stream_key, shape, shards, -0.22, 0.18) * result
    return jnp.clip(result, min=-most, max=most).astype(kind)


def setup_inputs(seed: int = 0) -> dict:
    arg_keys = jax.random.split(jax.random.key(seed), 7)
    leaf_density = scatter_about(arg_keys[0], (CELLS, P_SIZE), 1.0, 6.0, ((0, 128),))
    m2l_matrices = scatter_about(arg_keys[1], (NOFF, P_SIZE, P_SIZE), (P_SIZE * NOFF) ** -0.5, 0.03125)
    m2m_matrices = scatter_about(arg_keys[2], (8, P_SIZE, P_SIZE), (8 * P_SIZE) ** -0.5, 0.15625)
    send_index = touch_ends(jax.random.randint(arg_keys[3], (DEVICES, DEVICES, CAP), 0, C), jax.random.fold_in(arg_keys[3], 1), 0, C - 1).astype(jnp.int32)
    leaf_source = draw_leaf_source(jax.random.fold_in(arg_keys[6], 71), 0)
    coarse_source = draw_coarse_source(jax.random.fold_in(arg_keys[6], 71), 0)
    return {"leaf_density": leaf_density, "m2l_matrices": m2l_matrices, "m2m_matrices": m2m_matrices, "send_index": send_index, "leaf_source": leaf_source, "coarse_source": coarse_source}


def translate(table, index, kmat):
    nblk = index.shape[0] // 27
    blocks = index.reshape(nblk, 27, index.shape[1])
    mats = kmat.reshape(nblk, 27, kmat.shape[1], kmat.shape[2])

    def step(total, pair):
        rows = jnp.take(table, pair[0], axis=0).astype(jnp.float32)
        return total + jnp.einsum('otp,opq->tq', rows, pair[1].astype(jnp.float32)), None

    start = jnp.zeros((index.shape[1], kmat.shape[2]), jnp.float32)
    total, _ = lax.scan(step, start, (blocks, mats))
    return total


def reference(leaf_density, m2l_matrices, m2m_matrices, send_index, leaf_source, coarse_source):
    zero_row = jnp.zeros((1, P_SIZE), jnp.bfloat16)
    table = jnp.concatenate([leaf_density, zero_row], axis=0)
    device = (jnp.arange(CELLS, dtype=jnp.int32) // C)[None, :]
    src = leaf_source
    ghost = jnp.maximum(src - C, 0)
    peer = ghost // CAP
    slot = ghost % CAP
    flat = send_index.reshape(-1)
    far = peer * C + jnp.take(flat, ((peer * DEVICES + device) * CAP + slot).astype(jnp.int32))
    glob = jnp.where(src < 0, CELLS, jnp.where(src < C, device * C + src, far)).astype(jnp.int32)
    per_dev = glob.reshape(NOFF, DEVICES, C).transpose(1, 0, 2)
    leaf_local = lax.map(lambda idx: translate(table, idx, m2l_matrices), per_dev).reshape(CELLS, P_SIZE)
    parents = jnp.dot(leaf_density.reshape(NPAR, 8 * P_SIZE), m2m_matrices.reshape(8 * P_SIZE, P_SIZE),
                      preferred_element_type=jnp.float32).astype(jnp.bfloat16)
    table_two = jnp.concatenate([parents, zero_row], axis=0)
    cidx = jnp.where(coarse_source < 0, NPAR, coarse_source).astype(jnp.int32)
    cidx = cidx.reshape(NOFF, DEVICES, C // 8).transpose(1, 0, 2)
    coarse_local = 0.5 * lax.map(lambda idx: translate(table_two, idx, m2l_matrices), cidx).reshape(NPAR, P_SIZE)
    return leaf_local, parents, coarse_local
```

```python
import functools

import jax, jax.numpy as jnp
from jax import lax
from jax.experimental import pallas as pl
from jax.experimental.pallas import tpu as pltpu
from jax.sharding import PartitionSpec as P

LANES = 128


def translate_kernel(leaves, tail, idx_hbm, m2l_ref, leaf_ref, far_ref, near_ref, out_leaf, out_coarse,
                     table, acc, idx_vmem, f0, f1, f2, w0, w1, w2, s0, s1, s2, sem, vsem):
    step = pl.program_id(0)
    steps = pl.num_programs(0)
    rows_f = (f0, f1, f2)
    mats = (w0, w1, w2)
    smem = (s0, s1, s2)
    count = leaves + tail
    width = m2l_ref.shape[1]

    def fetch(k, s):
        return pltpu.make_async_copy(idx_vmem.at[3 * s + k], smem[k], sem.at[k])

    def gather(k):
        for t in range(count):
            i = smem[k][t // LANES, t % LANES]
            rows_f[k][pl.ds(2 * t, 2), :] = table[pl.ds(i, 2), :]

    def multiply(k):
        low = rows_f[k][pl.ds(0, count, stride=2), :].astype(jnp.bfloat16)
        high = rows_f[k][pl.ds(1, count, stride=2), :].astype(jnp.bfloat16)
        acc[...] += jnp.dot(jnp.concatenate([low, high], axis=1), mats[k][...], preferred_element_type=jnp.float32)

    def load_matrix(k):
        mats[k][0:width, 0:width] = m2l_ref[k]

    @pl.when(step == 0)
    def _():
        copy = pltpu.make_async_copy(idx_hbm, idx_vmem, vsem)
        copy.start()
        acc[...] = jnp.zeros_like(acc)
        f2[...] = jnp.zeros_like(f2)
        for w in mats:
            w[...] = jnp.zeros_like(w)
        table[0:8, :] = jnp.zeros((8, LANES), jnp.float32)
        place = 8
        for ref in (leaf_ref, far_ref, near_ref):
            n = ref.shape[0]
            block = 256
            start = place

            @pl.loop(0, n // block)
            def _(b):
                src = pl.ds(pl.multiple_of(b * block, block), block)
                dst = pl.ds(pl.multiple_of(start + b * block, 8), block)
                table[dst, :] = ref[src, :].astype(jnp.float32)
            place += n
        copy.wait()
        for k in range(3):
            fetch(k, 0).start()

    fetch(0, step).wait()
    gather(0)
    multiply(2)

    @pl.when(step + 1 < steps)
    def _():
        fetch(0, step + 1).start()
    for k in range(3):
        load_matrix(k)
    fetch(1, step).wait()
    gather(1)
    multiply(0)

    @pl.when(step + 1 < steps)
    def _():
        fetch(1, step + 1).start()
    fetch(2, step).wait()
    gather(2)
    multiply(1)

    @pl.when(step + 1 < steps)
    def _():
        fetch(2, step + 1).start()

    @pl.when(step == steps - 1)
    def _():
        multiply(2)
        out_leaf[...] = acc[0:leaves, 0:width]
        out_coarse[...] = 0.5 * acc[leaves:count, 0:width]


def translate(idx, m2l, leaf2, far2, near2, leaves, tail):
    noff, width, _ = m2l.shape
    count = leaves + tail
    whole = lambda ref: pl.BlockSpec(ref.shape, lambda s: (0,) * ref.ndim, pipeline_mode=pl.Buffered(1))
    rows = 8 + leaf2.shape[0] + far2.shape[0] + near2.shape[0]
    return pl.pallas_call(
        functools.partial(translate_kernel, leaves, tail),
        grid=(noff // 3,),
        in_specs=[
            pl.BlockSpec(memory_space=pl.ANY),
            pl.BlockSpec((3, width, width), lambda s: (s, 0, 0)),
            whole(leaf2), whole(far2), whole(near2),
        ],
        out_specs=[
            pl.BlockSpec((leaves, width), lambda s: (0, 0)),
            pl.BlockSpec((tail, width), lambda s: (0, 0)),
        ],
        out_shape=[
            jax.ShapeDtypeStruct((leaves, width), jnp.float32),
            jax.ShapeDtypeStruct((tail, width), jnp.float32),
        ],
        scratch_shapes=[
            pltpu.VMEM((rows, LANES), jnp.float32),
            pltpu.VMEM((count, 2 * LANES), jnp.float32),
            pltpu.VMEM(idx.shape, jnp.int32),
        ] + [pltpu.VMEM((2 * count, LANES), jnp.float32)] * 3
        + [pltpu.VMEM((2 * LANES, 2 * LANES), jnp.bfloat16)] * 3
        + [pltpu.SMEM(idx.shape[1:], jnp.int32)] * 3
        + [pltpu.SemaphoreType.DMA((3,)), pltpu.SemaphoreType.DMA],
        compiler_params=pltpu.CompilerParams(vmem_limit_bytes=58 * 2**20),
        cost_estimate=pl.CostEstimate(flops=2 * noff * count * width * width, bytes_accessed=20 * 2**20, transcendentals=0),
    )(idx, m2l, leaf2, far2, near2)


def pick_kernel(block, idx_ref, cells_ref, out_ref, table, rows_f):
    @pl.when(pl.program_id(0) == 0)
    def _():
        table[...] = cells_ref[...].astype(jnp.float32)

    @pl.loop(0, block // LANES)
    def _(r):
        row = idx_ref.at[pl.program_id(0) * (block // LANES) + r]
        base = pl.multiple_of(r * 2 * LANES, 2 * LANES)
        for u in range(LANES):
            rows_f[pl.ds(2 * u, 2), :] = table[pl.ds(row[u], 2), :]
        out_ref[pl.ds(base, 2 * LANES), :] = rows_f[...].astype(jnp.bfloat16)


def pick_rows(leaf2, chosen):
    devices, capacity = chosen.shape
    block = 16 * LANES
    total = devices * capacity
    return pl.pallas_call(
        functools.partial(pick_kernel, block),
        grid=(total // block,),
        in_specs=[
            pl.BlockSpec(memory_space=pltpu.SMEM),
            pl.BlockSpec(leaf2.shape, lambda s: (0, 0)),
        ],
        out_specs=pl.BlockSpec((2 * block, LANES), lambda s: (s, 0)),
        out_shape=jax.ShapeDtypeStruct((2 * total, LANES), jnp.bfloat16),
        scratch_shapes=[
            pltpu.VMEM(leaf2.shape, jnp.float32),
            pltpu.VMEM((2 * LANES, LANES), jnp.float32),
        ],
        compiler_params=pltpu.CompilerParams(vmem_limit_bytes=32 * 2**20),
        cost_estimate=pl.CostEstimate(flops=0, bytes_accessed=12 * 2**20, transcendentals=0),
    )(2 * chosen.reshape(total // LANES, LANES), leaf2)


def two_rows(x):
    return jnp.pad(x, ((0, 0), (0, 2 * LANES - x.shape[1]))).reshape(2 * x.shape[0], LANES)


def local(leaf_density, m2l_matrices, m2m_matrices, send_index, leaf_source, coarse_source):
    cells, width = leaf_density.shape
    noff = m2l_matrices.shape[0]
    parents_here = cells // 8
    devices, capacity = send_index.shape[1:]
    narrow = lax.axis_size("narrow")
    wide = lax.axis_size("wide")
    parents = jnp.dot(
        leaf_density.reshape(parents_here, 8 * width),
        m2m_matrices.reshape(8 * width, width),
        preferred_element_type=jnp.float32,
    ).astype(jnp.bfloat16)
    own = two_rows(parents)
    up = [(i, i + 1) for i in range(wide - 1)]
    down = [(j, i) for i, j in up]
    before = lax.ppermute(own, "wide", up)
    after = lax.ppermute(own, "wide", down)
    near = lax.all_gather(jnp.concatenate([before, own, after], axis=0), "narrow", axis=0, tiled=True)

    leaf2 = two_rows(leaf_density)
    outgoing = pick_rows(leaf2, send_index[0])
    far = lax.all_to_all(outgoing, ("wide", "narrow"), split_axis=0, concat_axis=0, tiled=True)

    group_rows = narrow * parents_here
    rel = coarse_source - (lax.axis_index("wide") - 1) * group_rows
    group, inside = rel // group_rows, rel % group_rows
    slot = (inside // parents_here) * (3 * parents_here) + group * parents_here + inside % parents_here
    coarse_row = jnp.where(coarse_source < 0, 0, 8 + 2 * (cells + devices * capacity + slot))
    leaf_row = jnp.where(leaf_source < 0, 0, 8 + 2 * leaf_source)
    used = cells + parents_here
    lines = -(-used // (8 * LANES)) * 8
    index = jnp.concatenate(
        [leaf_row, coarse_row, jnp.zeros((noff, lines * LANES - used), jnp.int32)], axis=1
    ).reshape(noff, lines, LANES)
    leaf_local, coarse_local = translate(index, m2l_matrices, leaf2, far, near, cells, parents_here)
    return (leaf_local, parents, coarse_local)


def solution(mesh):
    rows = P(("wide", "narrow"), None)
    columns = P(None, ("wide", "narrow"))
    return jax.shard_map(
        local,
        mesh=mesh,
        in_specs=(rows, P(), P(), P(("wide", "narrow"), None, None), columns, columns),
        out_specs=(rows, rows, rows),
        check_vma=False,
    )
```

```python
import functools

import jax
import jax.numpy as jnp
from jax import lax
from jax.experimental import pallas as pl
from jax.experimental.pallas import tpu as pltpu
from jax.sharding import PartitionSpec as P

LANES = 128
SPLIT = 4
RING = 3
ZERO = 8
PARTS = 8


def place_far(block, table, base):
    count = block.shape[0] - LANES // SPLIT
    rows, step = count // SPLIT, LANES // SPLIT
    table[pl.ds(base, count, stride=2), :] = block[0:count].astype(jnp.float32)
    rest = block[count:].astype(jnp.float32)
    for j in range(SPLIT):
        part = rest if j == 0 else pltpu.roll(rest, LANES - j * step, axis=1)
        table[pl.ds(base + 1 + 2 * j * rows, rows, stride=2), :] = part


def translate_kernel(group, count, scale, packed, halves, idx_hbm, m2l_ref, *refs):
    near_ref, refs = refs[0], refs[1:]
    if packed:
        far_hbm, refs = refs[0], refs[1:]
    out_ref, table, acc, idx_vmem = refs[:4]
    rows_f, mats, smem = refs[4:7], refs[7:10], refs[10:13]
    sem, vsem = refs[13:15]
    step = pl.program_id(0)
    steps = pl.num_programs(0)
    width = m2l_ref.shape[1]
    total = group * count

    def fetch(k, s):
        return pltpu.make_async_copy(idx_vmem.at[RING * s + k], smem[k], sem.at[k])

    def gather(k, lo, hi):
        for t in range(lo, hi):
            i = smem[k][t // LANES, t % LANES]
            rows_f[k][pl.ds(2 * t, 2), :] = table[pl.ds(i, 2), :]

    def multiply(k, lo, hi):
        n = min(hi - lo, count)
        at = lo % count if group > 1 else lo
        result = acc[at:at + n]
        for g in range(lo // count, -(-hi // count)):
            first = 2 * max(lo, g * count)
            low = rows_f[k][pl.ds(first, n, stride=2), :].astype(jnp.bfloat16)
            high = rows_f[k][pl.ds(first + 1, n, stride=2), :].astype(jnp.bfloat16)
            result += jnp.dot(jnp.concatenate([low, high], axis=1), mats[k][g], preferred_element_type=jnp.float32)
        acc[at:at + n] = result

    def load_matrix(k):
        for g in range(group):
            mats[k][g, 0:width, 0:width] = m2l_ref[k * group + g]

    @pl.when(step == 0)
    def _():
        copy = pltpu.make_async_copy(idx_hbm, idx_vmem, vsem)
        copy.start()
        if packed:
            far, fsem = refs[15:17]
            span = far.shape[0] // PARTS

            def part(q):
                return pltpu.make_async_copy(far_hbm.at[pl.ds(q * span, span)], far.at[pl.ds(q * span, span)], fsem.at[q])

            for q in range(PARTS):
                part(q).start()
        acc[...] = jnp.zeros_like(acc)
        rows_f[RING - 1][...] = jnp.zeros_like(rows_f[RING - 1])
        for w in mats:
            w[...] = jnp.zeros_like(w)
        table[0:ZERO, :] = jnp.zeros((ZERO, LANES), jnp.float32)
        n = near_ref.shape[0]
        table[pl.ds(ZERO, n), :] = near_ref[...].astype(jnp.float32)
        if packed:
            for q in range(PARTS):
                part(q).wait()

                @pl.loop(0, span)
                def _(b):
                    p = q * span + b
                    place_far(far[p], table, pl.multiple_of(ZERO + n + p * 2 * (far.shape[1] - LANES // SPLIT), 8))
        copy.wait()
        for k in range(RING):
            fetch(k, 0).start()

    for k in range(RING):
        fetch(k, step).wait()
        if k == 1:
            for j in range(RING):
                load_matrix(j)
        for lo, hi in zip(halves, halves[1:]):
            gather(k, lo, hi)
            multiply((k + RING - 1) % RING, lo, hi)

        @pl.when(step + 1 < steps)
        def _():
            fetch(k, step + 1).start()

    @pl.when(step == steps - 1)
    def _():
        for lo, hi in zip(halves, halves[1:]):
            multiply(RING - 1, lo, hi)
        out_ref[...] = scale * acc[:, 0:width] if scale != 1 else acc[:, 0:width]


def translate(idx, m2l, near2, far, group, count, scale, halves):
    noff, width, _ = m2l.shape
    rows = ZERO + near2.shape[0]
    total = group * count
    operands = [idx, m2l, near2]
    in_specs = [
        pl.BlockSpec(memory_space=pl.ANY),
        pl.BlockSpec((RING * group, width, width), lambda s: (s, 0, 0)),
        pl.BlockSpec(near2.shape, lambda s: (0, 0), pipeline_mode=pl.Buffered(1)),
    ]
    extra = []
    if far is not None:
        rows += 2 * far.shape[0] * (far.shape[1] - LANES // SPLIT)
        operands.append(far)
        in_specs.append(pl.BlockSpec(memory_space=pl.ANY))
        extra = [pltpu.VMEM(far.shape, far.dtype), pltpu.SemaphoreType.DMA((PARTS,))]
    return pl.pallas_call(
        functools.partial(translate_kernel, group, count, scale, far is not None, halves),
        grid=(noff // (RING * group),),
        in_specs=in_specs,
        out_specs=pl.BlockSpec((count, width), lambda s: (0, 0)),
        out_shape=jax.ShapeDtypeStruct((count, width), jnp.float32),
        scratch_shapes=[
            pltpu.VMEM((rows, LANES), jnp.float32),
            pltpu.VMEM((count, 2 * LANES), jnp.float32),
            pltpu.VMEM(idx.shape, jnp.int32),
        ] + [pltpu.VMEM((2 * total, LANES), jnp.float32)] * RING
        + [pltpu.VMEM((group, 2 * LANES, 2 * LANES), jnp.bfloat16)] * RING
        + [pltpu.SMEM(idx.shape[1:], jnp.int32)] * RING
        + [pltpu.SemaphoreType.DMA((RING,)), pltpu.SemaphoreType.DMA] + extra,
        compiler_params=pltpu.CompilerParams(vmem_limit_bytes=(50 if far is not None else 32) * 2**20),
        cost_estimate=pl.CostEstimate(
            flops=2 * noff * count * 256 * 256 * 3, bytes_accessed=20 * 2**20, transcendentals=0),
    )(*operands)


def pick_kernel(capacity, idx_hbm, cells_ref, out_ref, table, f0, f1, s0, s1, sem):
    step = pl.program_id(0)
    steps = pl.num_programs(0)
    rows_f, smem = (f0, f1), (s0, s1)
    lines = s0.shape[0]
    rows, lane = capacity // SPLIT, LANES // SPLIT

    def fetch(k, s):
        return pltpu.make_async_copy(idx_hbm.at[pl.ds((2 * s + k) * lines, lines)], smem[k], sem.at[k])

    @pl.when(step == 0)
    def _():
        for k in range(2):
            fetch(k, 0).start()
        table[...] = cells_ref[...].astype(jnp.float32)

    for k in range(2):
        fetch(k, step).wait()
        for r in range(lines):
            for u in range(capacity):
                rows_f[k][pl.ds(2 * (r * capacity + u), 2), :] = table[pl.ds(smem[k][r, u], 2), :]
            base = 2 * r * capacity
            out_ref[k * lines + r, 0:capacity] = rows_f[k][pl.ds(base, capacity, stride=2), :].astype(jnp.bfloat16)
            rest = rows_f[k][pl.ds(base + 1, rows, stride=2), :]
            for j in range(1, SPLIT):
                part = rows_f[k][pl.ds(base + 1 + 2 * j * rows, rows, stride=2), :]
                rest += pltpu.roll(part, j * lane, axis=1)
            out_ref[k * lines + r, capacity:] = rest.astype(jnp.bfloat16)

        @pl.when(step + 1 < steps)
        def _():
            fetch(k, step + 1).start()


def pick_rows(leaf2, chosen):
    devices, capacity = chosen.shape
    lines = 8
    return pl.pallas_call(
        functools.partial(pick_kernel, capacity),
        grid=(devices // (2 * lines),),
        in_specs=[
            pl.BlockSpec(memory_space=pl.ANY),
            pl.BlockSpec(leaf2.shape, lambda s: (0, 0)),
        ],
        out_specs=pl.BlockSpec((2 * lines, capacity + capacity // SPLIT, LANES), lambda s: (s, 0, 0)),
        out_shape=jax.ShapeDtypeStruct((devices, capacity + capacity // SPLIT, LANES), jnp.bfloat16),
        scratch_shapes=[pltpu.VMEM(leaf2.shape, jnp.float32)]
        + [pltpu.VMEM((2 * lines * capacity, LANES), jnp.float32)] * 2
        + [pltpu.SMEM((lines, capacity), jnp.int32)] * 2
        + [pltpu.SemaphoreType.DMA((2,))],
        compiler_params=pltpu.CompilerParams(vmem_limit_bytes=32 * 2**20),
        cost_estimate=pl.CostEstimate(flops=0, bytes_accessed=32 * 2**20, transcendentals=0),
    )(2 * chosen, leaf2)


def two_rows(x):
    return jnp.pad(x, ((0, 0), (0, 2 * LANES - x.shape[1]))).reshape(2 * x.shape[0], LANES)


def lines_of(index):
    used = index.shape[1]
    lines = -(-used // LANES)
    return jnp.pad(index, ((0, 0), (0, lines * LANES - used))).reshape(index.shape[0], lines, LANES)


def local(leaf_density, m2l_matrices, m2m_matrices, send_index, leaf_source, coarse_source):
    cells, width = leaf_density.shape
    noff = m2l_matrices.shape[0]
    parents_here = cells // 8
    narrow = lax.axis_size("narrow")
    wide = lax.axis_size("wide")
    parents = jnp.dot(
        leaf_density.reshape(parents_here, 8 * width),
        m2m_matrices.reshape(8 * width, width),
        preferred_element_type=jnp.float32,
    ).astype(jnp.bfloat16)
    own = two_rows(parents)
    up = [(i, i + 1) for i in range(wide - 1)]
    down = [(j, i) for i, j in up]
    before = lax.ppermute(own, "wide", up)
    after = lax.ppermute(own, "wide", down)
    near = lax.all_gather(jnp.concatenate([before, own, after], axis=0), "narrow", axis=0, tiled=True)

    leaf2 = two_rows(leaf_density)
    outgoing = pick_rows(leaf2, send_index[0])
    outgoing, near, m2l_matrices, leaf_source, coarse_source = lax.optimization_barrier(
        (outgoing, near, m2l_matrices, leaf_source, coarse_source)
    )
    far = lax.all_to_all(outgoing, ("wide", "narrow"), split_axis=0, concat_axis=0, tiled=True)

    group_rows = narrow * parents_here
    rel = coarse_source - (lax.axis_index("wide") - 1) * group_rows
    group, inside = rel // group_rows, rel % group_rows
    slot = (inside // parents_here) * (3 * parents_here) + group * parents_here + inside % parents_here
    coarse_row = jnp.where(coarse_source < 0, 0, ZERO + 2 * slot)
    together = 9
    coarse_index = lines_of(coarse_row.reshape(noff // together, together * parents_here))
    bounds = tuple(together * parents_here * h // 3 for h in range(4))
    coarse_local = translate(coarse_index, m2l_matrices, near, None, together, parents_here, 0.5, bounds)

    leaf_index = lines_of(jnp.where(leaf_source < 0, 0, ZERO + 2 * leaf_source))
    far, leaf_index, coarse_local = lax.optimization_barrier((far, leaf_index, coarse_local))
    leaf_local = translate(leaf_index, m2l_matrices, leaf2, far, 1, cells, 1, (0, cells // 2, cells))
    return (leaf_local, parents, coarse_local)


def solution(mesh):
    rows = P(("wide", "narrow"), None)
    columns = P(None, ("wide", "narrow"))
    return jax.shard_map(
        local,
        mesh=mesh,
        in_specs=(rows, P(), P(), P(("wide", "narrow"), None, None), columns, columns),
        out_specs=(rows, rows, rows),
        check_vma=False,
    )
```

```python
import functools

import jax
import jax.numpy as jnp
from jax import lax
from jax.experimental import pallas as pl
from jax.experimental.pallas import tpu as pltpu
from jax.sharding import PartitionSpec as P

LANES = 128
SPLIT = 4
RING = 3
ZERO = 8
PARTS = 8
LEAF_GROUP = 1
LEAF_BURST = 9
LEAF_PIECES = 2


def place_far(block, table, base):
    count = block.shape[0] - LANES // SPLIT
    rows, step = count // SPLIT, LANES // SPLIT
    table[pl.ds(base, count, stride=2), :] = block[0:count].astype(jnp.float32)
    rest = block[count:].astype(jnp.float32)
    for j in range(SPLIT):
        part = rest if j == 0 else pltpu.roll(rest, LANES - j * step, axis=1)
        table[pl.ds(base + 1 + 2 * j * rows, rows, stride=2), :] = part


def translate_kernel(group, count, scale, packed, burst, pieces, idx_hbm, m2l_ref, *refs):
    near_ref, refs = refs[0], refs[1:]
    if packed:
        far_hbm, refs = refs[0], refs[1:]
    out_ref, table, acc, idx_vmem = refs[:4]
    rows_f, mats, smem = refs[4:7], refs[7:10], refs[10:13]
    sem, vsem = refs[13:15]
    step = pl.program_id(0)
    steps = pl.num_programs(0)
    width = m2l_ref.shape[1]
    total = group * count

    def fetch(k, c):
        return pltpu.make_async_copy(idx_vmem.at[c], smem[k], sem.at[k])

    def gather(k, lo, hi):
        for t in range(lo, hi):
            i = smem[k][t // LANES, t % LANES]
            rows_f[k][pl.ds(2 * t, 2), :] = table[pl.ds(i, 2), :]

    def multiply(k, lo, hi):
        sides = []
        for g in range(group):
            for side in range(2):
                rows = pl.ds(2 * (g * count + lo) + side, hi - lo, stride=2)
                sides.append(rows_f[k][rows, :].astype(jnp.bfloat16))
        acc[lo:hi] += jnp.dot(jnp.concatenate(sides, axis=1), mats[k][...], preferred_element_type=jnp.float32)

    def load_matrix(k, c):
        for g in range(group):
            mats[k][2 * LANES * g:2 * LANES * g + width, 0:width] = m2l_ref[c * group + g]

    @pl.when(step == 0)
    def _():
        copy = pltpu.make_async_copy(idx_hbm, idx_vmem, vsem)
        copy.start()
        if packed:
            far, fsem = refs[15:17]
            span = far.shape[0] // PARTS

            def part(q):
                return pltpu.make_async_copy(far_hbm.at[pl.ds(q * span, span)], far.at[pl.ds(q * span, span)], fsem.at[q])

            for q in range(PARTS):
                part(q).start()
        acc[...] = jnp.zeros_like(acc)
        last = rows_f[(burst - 1) % RING]
        last[...] = jnp.zeros_like(last)
        for w in mats:
            w[...] = jnp.zeros_like(w)
        table[0:ZERO, :] = jnp.zeros((ZERO, LANES), jnp.float32)
        n = near_ref.shape[0]
        table[pl.ds(ZERO, n), :] = near_ref[...].astype(jnp.float32)
        if packed:
            for q in range(PARTS):
                part(q).wait()

                @pl.loop(0, span)
                def _(b):
                    p = q * span + b
                    place_far(far[p], table, pl.multiple_of(ZERO + n + p * 2 * (far.shape[1] - LANES // SPLIT), 8))
        copy.wait()
        for k in range(RING):
            fetch(k, k).start()

    for c in range(burst):
        k = c % RING
        fetch(k, burst * step + c).wait()
        load_matrix(k, c)
        for p in range(pieces):
            gather(k, total * p // pieces, total * (p + 1) // pieces)
            multiply((c + burst - 1) % burst % RING, count * p // pieces, count * (p + 1) // pieces)

        @pl.when(burst * step + c + RING < burst * steps)
        def _():
            fetch(k, burst * step + c + RING).start()

    @pl.when(step == steps - 1)
    def _():
        multiply((burst - 1) % RING, 0, count)
        out_ref[...] = scale * acc[:, 0:width] if scale != 1 else acc[:, 0:width]


def translate(idx, m2l, near2, far, group, count, scale, burst, pieces):
    noff, width, _ = m2l.shape
    rows = ZERO + near2.shape[0]
    total = group * count
    operands = [idx, m2l, near2]
    in_specs = [
        pl.BlockSpec(memory_space=pl.ANY),
        pl.BlockSpec((burst * group, width, width), lambda s: (s, 0, 0)),
        pl.BlockSpec(near2.shape, lambda s: (0, 0), pipeline_mode=pl.Buffered(1)),
    ]
    extra = []
    if far is not None:
        rows += 2 * far.shape[0] * (far.shape[1] - LANES // SPLIT)
        operands.append(far)
        in_specs.append(pl.BlockSpec(memory_space=pl.ANY))
        extra = [pltpu.VMEM(far.shape, far.dtype), pltpu.SemaphoreType.DMA((PARTS,))]
    return pl.pallas_call(
        functools.partial(translate_kernel, group, count, scale, far is not None, burst, pieces),
        grid=(noff // (burst * group),),
        in_specs=in_specs,
        out_specs=pl.BlockSpec((count, width), lambda s: (0, 0)),
        out_shape=jax.ShapeDtypeStruct((count, width), jnp.float32),
        scratch_shapes=[
            pltpu.VMEM((rows, LANES), jnp.float32),
            pltpu.VMEM((count, 2 * LANES), jnp.float32),
            pltpu.VMEM(idx.shape, jnp.int32),
        ] + [pltpu.VMEM((2 * total, LANES), jnp.float32)] * RING
        + [pltpu.VMEM((group * 2 * LANES, 2 * LANES), jnp.bfloat16)] * RING
        + [pltpu.SMEM(idx.shape[1:], jnp.int32)] * RING
        + [pltpu.SemaphoreType.DMA((RING,)), pltpu.SemaphoreType.DMA] + extra,
        compiler_params=pltpu.CompilerParams(vmem_limit_bytes=56 * 2**20),
        cost_estimate=pl.CostEstimate(
            flops=2 * noff * count * 256 * 256 * 3, bytes_accessed=20 * 2**20, transcendentals=0),
    )(*operands)


def pick_kernel(capacity, idx_hbm, cells_ref, out_ref, table, f0, f1, s0, s1, sem):
    step = pl.program_id(0)
    steps = pl.num_programs(0)
    rows_f, smem = (f0, f1), (s0, s1)
    lines = s0.shape[0]
    rows, lane = capacity // SPLIT, LANES // SPLIT

    def fetch(k, s):
        return pltpu.make_async_copy(idx_hbm.at[pl.ds((2 * s + k) * lines, lines)], smem[k], sem.at[k])

    @pl.when(step == 0)
    def _():
        for k in range(2):
            fetch(k, 0).start()
        table[...] = cells_ref[...].astype(jnp.float32)

    for k in range(2):
        fetch(k, step).wait()
        for r in range(lines):
            for u in range(capacity):
                rows_f[k][pl.ds(2 * (r * capacity + u), 2), :] = table[pl.ds(smem[k][r, u], 2), :]
            base = 2 * r * capacity
            out_ref[k * lines + r, 0:capacity] = rows_f[k][pl.ds(base, capacity, stride=2), :].astype(jnp.bfloat16)
            rest = rows_f[k][pl.ds(base + 1, rows, stride=2), :]
            for j in range(1, SPLIT):
                part = rows_f[k][pl.ds(base + 1 + 2 * j * rows, rows, stride=2), :]
                rest += pltpu.roll(part, j * lane, axis=1)
            out_ref[k * lines + r, capacity:] = rest.astype(jnp.bfloat16)

        @pl.when(step + 1 < steps)
        def _():
            fetch(k, step + 1).start()


def pick_rows(leaf2, chosen):
    devices, capacity = chosen.shape
    lines = 8
    return pl.pallas_call(
        functools.partial(pick_kernel, capacity),
        grid=(devices // (2 * lines),),
        in_specs=[
            pl.BlockSpec(memory_space=pl.ANY),
            pl.BlockSpec(leaf2.shape, lambda s: (0, 0)),
        ],
        out_specs=pl.BlockSpec((2 * lines, capacity + capacity // SPLIT, LANES), lambda s: (s, 0, 0)),
        out_shape=jax.ShapeDtypeStruct((devices, capacity + capacity // SPLIT, LANES), jnp.bfloat16),
        scratch_shapes=[pltpu.VMEM(leaf2.shape, jnp.float32)]
        + [pltpu.VMEM((2 * lines * capacity, LANES), jnp.float32)] * 2
        + [pltpu.SMEM((lines, capacity), jnp.int32)] * 2
        + [pltpu.SemaphoreType.DMA((2,))],
        compiler_params=pltpu.CompilerParams(vmem_limit_bytes=56 * 2**20),
        cost_estimate=pl.CostEstimate(flops=0, bytes_accessed=32 * 2**20, transcendentals=0),
    )(2 * chosen, leaf2)


def two_rows(x):
    return jnp.pad(x, ((0, 0), (0, 2 * LANES - x.shape[1]))).reshape(2 * x.shape[0], LANES)


def lines_of(index):
    used = index.shape[1]
    lines = -(-used // LANES)
    return jnp.pad(index, ((0, 0), (0, lines * LANES - used))).reshape(index.shape[0], lines, LANES)


def local(leaf_density, m2l_matrices, m2m_matrices, send_index, leaf_source, coarse_source):
    cells, width = leaf_density.shape
    noff = m2l_matrices.shape[0]
    parents_here = cells // 8
    narrow = lax.axis_size("narrow")
    wide = lax.axis_size("wide")
    parents = jnp.dot(
        leaf_density.reshape(parents_here, 8 * width),
        m2m_matrices.reshape(8 * width, width),
        preferred_element_type=jnp.float32,
    ).astype(jnp.bfloat16)
    own = two_rows(parents)
    up = [(i, i + 1) for i in range(wide - 1)]
    down = [(j, i) for i, j in up]
    before = lax.ppermute(own, "wide", up)
    after = lax.ppermute(own, "wide", down)
    three = jnp.concatenate([before, own, after], axis=0)
    near = lax.all_to_all(
        jnp.broadcast_to(three, (narrow,) + three.shape), "narrow", split_axis=0, concat_axis=0, tiled=True
    ).reshape(narrow * three.shape[0], LANES)

    leaf2 = two_rows(leaf_density)
    outgoing = pick_rows(leaf2, send_index[0])
    outgoing, near, m2l_matrices, leaf_source, coarse_source = lax.optimization_barrier(
        (outgoing, near, m2l_matrices, leaf_source, coarse_source)
    )
    far = lax.all_to_all(outgoing, ("wide", "narrow"), split_axis=0, concat_axis=0, tiled=True)

    group_rows = narrow * parents_here
    rel = coarse_source - (lax.axis_index("wide") - 1) * group_rows
    group, inside = rel // group_rows, rel % group_rows
    slot = (inside // parents_here) * (3 * parents_here) + group * parents_here + inside % parents_here
    coarse_row = jnp.where(coarse_source < 0, 0, ZERO + 2 * slot)
    together = 9
    coarse_index = lines_of(coarse_row.reshape(noff // together, together * parents_here))
    coarse_local = translate(coarse_index, m2l_matrices, near, None, together, parents_here, 0.5, 3, 1)

    leaf_index = lines_of(
        jnp.where(leaf_source < 0, 0, ZERO + 2 * leaf_source).reshape(noff // LEAF_GROUP, LEAF_GROUP * cells)
    )
    far, leaf_index, coarse_local = lax.optimization_barrier((far, leaf_index, coarse_local))
    leaf_local = translate(leaf_index, m2l_matrices, leaf2, far, LEAF_GROUP, cells, 1, LEAF_BURST, LEAF_PIECES)
    return (leaf_local, parents, coarse_local)


def solution(mesh):
    rows = P(("wide", "narrow"), None)
    columns = P(None, ("wide", "narrow"))
    return jax.shard_map(
        local,
        mesh=mesh,
        in_specs=(rows, P(), P(), P(("wide", "narrow"), None, None), columns, columns),
        out_specs=(rows, rows, rows),
        check_vma=False,
    )
```

```python
import functools

import jax
import jax.numpy as jnp
from jax import lax
from jax.experimental import pallas as pl
from jax.experimental.pallas import tpu as pltpu
from jax.sharding import PartitionSpec as P

LANES = 128
SPLIT = 4
RING = 3
ZERO = 8
PARTS = 8
LEAF_GROUP = 1
LEAF_BURST = 9
LEAF_PIECES = 2


def place_far(block, table, base):
    count = block.shape[0] - LANES // SPLIT
    rows, step = count // SPLIT, LANES // SPLIT
    table[pl.ds(base, count, stride=2), :] = block[0:count].astype(jnp.float32)
    rest = block[count:].astype(jnp.float32)
    for j in range(SPLIT):
        part = rest if j == 0 else pltpu.roll(rest, LANES - j * step, axis=1)
        table[pl.ds(base + 1 + 2 * j * rows, rows, stride=2), :] = part


def translate_kernel(group, count, scale, packed, burst, pieces, idx_hbm, m2l_ref, *refs):
    near_ref, refs = refs[0], refs[1:]
    if packed:
        far_hbm, refs = refs[0], refs[1:]
    out_ref, table, acc, idx_vmem = refs[:4]
    rows_f, mats, smem = refs[4:7], refs[7:10], refs[10:13]
    sem, vsem = refs[13:15]
    step = pl.program_id(0)
    steps = pl.num_programs(0)
    width = m2l_ref.shape[1]
    total = group * count

    def fetch(k, c):
        return pltpu.make_async_copy(idx_vmem.at[c], smem[k], sem.at[k])

    def gather(k, lo, hi):
        for t in range(lo, hi):
            i = smem[k][t // LANES, t % LANES]
            rows_f[k][pl.ds(2 * t, 2), :] = table[pl.ds(i, 2), :]

    def multiply(k, lo, hi):
        sides = []
        for g in range(group):
            for side in range(2):
                rows = pl.ds(2 * (g * count + lo) + side, hi - lo, stride=2)
                sides.append(rows_f[k][rows, :].astype(jnp.bfloat16))
        acc[lo:hi] += jnp.dot(jnp.concatenate(sides, axis=1), mats[k][...], preferred_element_type=jnp.float32)

    def load_matrix(k, c):
        for g in range(group):
            mats[k][2 * LANES * g:2 * LANES * g + width, 0:width] = m2l_ref[c * group + g]

    @pl.when(step == 0)
    def _():
        copy = pltpu.make_async_copy(idx_hbm, idx_vmem, vsem)
        copy.start()
        if packed:
            far, fsem = refs[15:17]
            span = far.shape[0] // PARTS

            def part(q):
                return pltpu.make_async_copy(far_hbm.at[pl.ds(q * span, span)], far.at[pl.ds(q * span, span)], fsem.at[q])

            for q in range(PARTS):
                part(q).start()
        acc[...] = jnp.zeros_like(acc)
        last = rows_f[(burst - 1) % RING]
        last[...] = jnp.zeros_like(last)
        for w in mats:
            w[...] = jnp.zeros_like(w)
        table[0:ZERO, :] = jnp.zeros((ZERO, LANES), jnp.float32)
        n = near_ref.shape[0]
        table[pl.ds(ZERO, n), :] = near_ref[...].astype(jnp.float32)
        if packed:
            for q in range(PARTS):
                part(q).wait()

                @pl.loop(0, span)
                def _(b):
                    p = q * span + b
                    place_far(far[p], table, pl.multiple_of(ZERO + n + p * 2 * (far.shape[1] - LANES // SPLIT), 8))
        copy.wait()
        for k in range(RING):
            fetch(k, k).start()

    for c in range(burst):
        k = c % RING
        fetch(k, burst * step + c).wait()
        load_matrix(k, c)
        for p in range(pieces):
            gather(k, total * p // pieces, total * (p + 1) // pieces)
            multiply((c + burst - 1) % burst % RING, count * p // pieces, count * (p + 1) // pieces)

        @pl.when(burst * step + c + RING < burst * steps)
        def _():
            fetch(k, burst * step + c + RING).start()

    @pl.when(step == steps - 1)
    def _():
        multiply((burst - 1) % RING, 0, count)
        total_t = acc[...].T[0:width]
        out_ref[...] = scale * total_t if scale != 1 else total_t


def translate(idx, m2l, near2, far, group, count, scale, burst, pieces):
    noff, width, _ = m2l.shape
    rows = ZERO + near2.shape[0]
    total = group * count
    operands = [idx, m2l, near2]
    in_specs = [
        pl.BlockSpec(memory_space=pl.ANY),
        pl.BlockSpec((burst * group, width, width), lambda s: (s, 0, 0)),
        pl.BlockSpec(near2.shape, lambda s: (0, 0), pipeline_mode=pl.Buffered(1)),
    ]
    extra = []
    if far is not None:
        rows += 2 * far.shape[0] * (far.shape[1] - LANES // SPLIT)
        operands.append(far)
        in_specs.append(pl.BlockSpec(memory_space=pl.ANY))
        extra = [pltpu.VMEM(far.shape, far.dtype), pltpu.SemaphoreType.DMA((PARTS,))]
    return pl.pallas_call(
        functools.partial(translate_kernel, group, count, scale, far is not None, burst, pieces),
        grid=(noff // (burst * group),),
        in_specs=in_specs,
        out_specs=pl.BlockSpec((width, count), lambda s: (0, 0)),
        out_shape=jax.ShapeDtypeStruct((width, count), jnp.float32),
        scratch_shapes=[
            pltpu.VMEM((rows, LANES), jnp.float32),
            pltpu.VMEM((count, 2 * LANES), jnp.float32),
            pltpu.VMEM(idx.shape, jnp.int32),
        ] + [pltpu.VMEM((2 * total, LANES), jnp.float32)] * RING
        + [pltpu.VMEM((group * 2 * LANES, 2 * LANES), jnp.bfloat16)] * RING
        + [pltpu.SMEM(idx.shape[1:], jnp.int32)] * RING
        + [pltpu.SemaphoreType.DMA((RING,)), pltpu.SemaphoreType.DMA] + extra,
        compiler_params=pltpu.CompilerParams(vmem_limit_bytes=56 * 2**20),
        cost_estimate=pl.CostEstimate(
            flops=2 * noff * count * 256 * 256 * 3, bytes_accessed=20 * 2**20, transcendentals=0),
    )(*operands).T


def pick_kernel(capacity, first, idx_hbm, cells_ref, *refs):
    out_ref, table, f0, f1, s0, s1, sem = refs[-7:]
    step = pl.program_id(0)
    steps = pl.num_programs(0)
    rows_f, smem = (f0, f1), (s0, s1)
    lines = s0.shape[0]
    rows, lane = capacity // SPLIT, LANES // SPLIT

    def fetch(k, s):
        return pltpu.make_async_copy(idx_hbm.at[pl.ds((2 * (first + s) + k) * lines, lines)], smem[k], sem.at[k])

    @pl.when(step == 0)
    def _():
        for k in range(2):
            fetch(k, 0).start()
        table[...] = cells_ref[...].astype(jnp.float32)

    for k in range(2):
        fetch(k, step).wait()
        for r in range(lines):
            for u in range(capacity):
                rows_f[k][pl.ds(2 * (r * capacity + u), 2), :] = table[pl.ds(smem[k][r, u], 2), :]
            base = 2 * r * capacity
            out_ref[k * lines + r, 0:capacity] = rows_f[k][pl.ds(base, capacity, stride=2), :].astype(jnp.bfloat16)
            rest = rows_f[k][pl.ds(base + 1, rows, stride=2), :]
            for j in range(1, SPLIT):
                part = rows_f[k][pl.ds(base + 1 + 2 * j * rows, rows, stride=2), :]
                rest += pltpu.roll(part, j * lane, axis=1)
            out_ref[k * lines + r, capacity:] = rest.astype(jnp.bfloat16)

        @pl.when(step + 1 < steps)
        def _():
            fetch(k, step + 1).start()


def pick_rows(leaf2, chosen, half, partial=None):
    devices, capacity = chosen.shape
    lines = 8
    steps = devices // (4 * lines)
    first = half * steps
    operands = [chosen, leaf2]
    in_specs = [pl.BlockSpec(memory_space=pl.ANY), pl.BlockSpec(leaf2.shape, lambda s: (0, 0))]
    if partial is not None:
        operands.append(partial)
        in_specs.append(pl.BlockSpec(memory_space=pl.ANY))
    return pl.pallas_call(
        functools.partial(pick_kernel, capacity, first),
        grid=(steps,),
        in_specs=in_specs,
        out_specs=pl.BlockSpec((2 * lines, capacity + capacity // SPLIT, LANES), lambda s: (first + s, 0, 0)),
        out_shape=jax.ShapeDtypeStruct((devices, capacity + capacity // SPLIT, LANES), jnp.bfloat16),
        scratch_shapes=[pltpu.VMEM(leaf2.shape, jnp.float32)]
        + [pltpu.VMEM((2 * lines * capacity, LANES), jnp.float32)] * 2
        + [pltpu.SMEM((lines, capacity), jnp.int32)] * 2
        + [pltpu.SemaphoreType.DMA((2,))],
        input_output_aliases={} if partial is None else {2: 0},
        compiler_params=pltpu.CompilerParams(vmem_limit_bytes=56 * 2**20),
        cost_estimate=pl.CostEstimate(flops=0, bytes_accessed=24 * 2**20, transcendentals=0),
    )(*operands)


def two_rows(x):
    return jnp.pad(x, ((0, 0), (0, 2 * LANES - x.shape[1]))).reshape(2 * x.shape[0], LANES)


def lines_of(index):
    used = index.shape[1]
    lines = -(-used // LANES)
    return jnp.pad(index, ((0, 0), (0, lines * LANES - used))).reshape(index.shape[0], lines, LANES)


def local(leaf_density, m2l_matrices, m2m_matrices, send_index, leaf_source, coarse_source):
    cells, width = leaf_density.shape
    noff = m2l_matrices.shape[0]
    parents_here = cells // 8
    narrow = lax.axis_size("narrow")
    wide = lax.axis_size("wide")
    parents = jnp.dot(
        leaf_density.reshape(parents_here, 8 * width),
        m2m_matrices.reshape(8 * width, width),
        preferred_element_type=jnp.float32,
    ).astype(jnp.bfloat16)
    own = two_rows(parents)
    group = lax.all_to_all(
        jnp.broadcast_to(own, (narrow,) + own.shape), "narrow", split_axis=0, concat_axis=0, tiled=True
    ).reshape(narrow * own.shape[0], LANES)

    leaf2 = two_rows(leaf_density)
    chosen = 2 * send_index[0]
    outgoing = pick_rows(leaf2, chosen, 0)
    outgoing, group = lax.optimization_barrier((outgoing, group))
    up = [(i, i + 1) for i in range(wide - 1)]
    down = [(j, i) for i, j in up]
    before = lax.ppermute(group, "wide", up)
    after = lax.ppermute(group, "wide", down)
    outgoing = pick_rows(leaf2, chosen, 1, outgoing)
    outgoing, before, after, m2l_matrices, leaf_source, coarse_source = lax.optimization_barrier(
        (outgoing, before, after, m2l_matrices, leaf_source, coarse_source)
    )
    far = lax.all_to_all(outgoing, ("wide", "narrow"), split_axis=0, concat_axis=0, tiled=True)

    near = jnp.concatenate([before, group, after], axis=0)
    base = (lax.axis_index("wide") - 1) * (narrow * parents_here)
    coarse_row = jnp.where(coarse_source < 0, 0, ZERO + 2 * (coarse_source - base))
    together = 9
    coarse_index = lines_of(coarse_row.reshape(noff // together, together * parents_here))
    coarse_local = translate(coarse_index, m2l_matrices, near, None, together, parents_here, 0.5, 3, 1)

    leaf_index = lines_of(
        jnp.where(leaf_source < 0, 0, ZERO + 2 * leaf_source).reshape(noff // LEAF_GROUP, LEAF_GROUP * cells)
    )
    far, leaf_index, coarse_local = lax.optimization_barrier((far, leaf_index, coarse_local))
    leaf_local = translate(leaf_index, m2l_matrices, leaf2, far, LEAF_GROUP, cells, 1, LEAF_BURST, LEAF_PIECES)
    return (leaf_local, parents, coarse_local)


def solution(mesh):
    rows = P(("wide", "narrow"), None)
    columns = P(None, ("wide", "narrow"))
    return jax.shard_map(
        local,
        mesh=mesh,
        in_specs=(rows, P(), P(), P(("wide", "narrow"), None, None), columns, columns),
        out_specs=(rows, rows, rows),
        check_vma=False,
    )
```

```python
import functools

import jax
import jax.numpy as jnp
from jax import lax
from jax.experimental import pallas as pl
from jax.experimental.pallas import tpu as pltpu
from jax.sharding import PartitionSpec as P

LANES = 128
SPLIT = 4
RING = 3
ZERO = 8
PARTS = 8
LEAF_GROUP = 1
LEAF_BURST = 9
LEAF_PIECES = 2


def place_far(block, table, base):
    count = block.shape[0] - LANES // SPLIT
    rows, step = count // SPLIT, LANES // SPLIT
    table[pl.ds(base, count, stride=2), :] = block[0:count].astype(jnp.float32)
    rest = block[count:].astype(jnp.float32)
    for j in range(SPLIT):
        part = rest if j == 0 else pltpu.roll(rest, LANES - j * step, axis=1)
        table[pl.ds(base + 1 + 2 * j * rows, rows, stride=2), :] = part


def translate_kernel(group, count, scale, packed, burst, pieces, idx_hbm, m2l_ref, *refs):
    near_ref, refs = refs[0], refs[1:]
    if packed:
        far_hbm, refs = refs[0], refs[1:]
    out_ref, table, acc, idx_vmem = refs[:4]
    rows_f, kept, smem = refs[4:7], refs[7], refs[8:11]
    sem, vsem = refs[11:13]
    step = pl.program_id(0)
    steps = pl.num_programs(0)
    width = m2l_ref.shape[1]
    total = group * count

    def fetch(k, c):
        return pltpu.make_async_copy(idx_vmem.at[c], smem[k], sem.at[k])

    def gather(k, lo, hi):
        for t in range(lo, hi):
            i = smem[k][t // LANES, t % LANES]
            rows_f[k][pl.ds(2 * t, 2), :] = table[pl.ds(i, 2), :]

    def multiply(k, lo, hi, matrix):
        sides = []
        for g in range(group):
            for side in range(2):
                rows = pl.ds(2 * (g * count + lo) + side, hi - lo, stride=2)
                sides.append(rows_f[k][rows, :].astype(jnp.bfloat16))
        acc[lo:hi] += jnp.dot(jnp.concatenate(sides, axis=1), matrix, preferred_element_type=jnp.float32)

    def matrix_of(c):
        room = 2 * LANES - width
        return jnp.concatenate([jnp.pad(m2l_ref[c * group + g], ((0, room), (0, room))) for g in range(group)], axis=0)

    @pl.when(step == 0)
    def _():
        copy = pltpu.make_async_copy(idx_hbm, idx_vmem, vsem)
        copy.start()
        if packed:
            far, fsem = refs[13:15]
            span = far.shape[0] // PARTS

            def part(q):
                return pltpu.make_async_copy(far_hbm.at[pl.ds(q * span, span)], far.at[pl.ds(q * span, span)], fsem.at[q])

            for q in range(PARTS):
                part(q).start()
        acc[...] = jnp.zeros_like(acc)
        last = rows_f[(burst - 1) % RING]
        last[...] = jnp.zeros_like(last)
        kept[...] = jnp.zeros_like(kept)
        table[0:ZERO, :] = jnp.zeros((ZERO, LANES), jnp.float32)
        copy.wait()
        for k in range(RING):
            fetch(k, k).start()
        n = near_ref.shape[0]
        if packed:
            place_cells(near_ref[...], table, ZERO)
            n = 2 * n
        else:
            table[pl.ds(ZERO, n), :] = near_ref[...].astype(jnp.float32)
        if packed:
            for q in range(PARTS):
                part(q).wait()

                @pl.loop(0, span)
                def _(b):
                    p = q * span + b
                    place_far(far[p], table, pl.multiple_of(ZERO + n + p * 2 * (far.shape[1] - LANES // SPLIT), 8))

    for c in range(burst):
        k = c % RING
        fetch(k, burst * step + c).wait()
        matrix = kept[...] if c == 0 else matrix_of(c - 1)
        for p in range(pieces):
            gather(k, total * p // pieces, total * (p + 1) // pieces)
            multiply((c + burst - 1) % burst % RING, count * p // pieces, count * (p + 1) // pieces, matrix)

        @pl.when(burst * step + c + RING < burst * steps)
        def _():
            fetch(k, burst * step + c + RING).start()

    kept[...] = matrix_of(burst - 1)

    @pl.when(step == steps - 1)
    def _():
        multiply((burst - 1) % RING, 0, count, kept[...])
        total_t = acc[...].T[0:width]
        out_ref[...] = scale * total_t if scale != 1 else total_t


def translate(idx, m2l, near2, far, group, count, scale, burst, pieces):
    noff, width, _ = m2l.shape
    rows = ZERO + near2.shape[0] * (1 if far is None else 2)
    total = group * count
    operands = [idx, m2l, near2]
    in_specs = [
        pl.BlockSpec(memory_space=pl.ANY),
        pl.BlockSpec((burst * group, width, width), lambda s: (s, 0, 0)),
        pl.BlockSpec(near2.shape, lambda s: (0, 0), pipeline_mode=pl.Buffered(1)),
    ]
    extra = []
    if far is not None:
        rows += 2 * far.shape[0] * (far.shape[1] - LANES // SPLIT)
        operands.append(far)
        in_specs.append(pl.BlockSpec(memory_space=pl.ANY))
        extra = [pltpu.VMEM(far.shape, far.dtype), pltpu.SemaphoreType.DMA((PARTS,))]
    return pl.pallas_call(
        functools.partial(translate_kernel, group, count, scale, far is not None, burst, pieces),
        grid=(noff // (burst * group),),
        in_specs=in_specs,
        out_specs=pl.BlockSpec((width, count), lambda s: (0, 0)),
        out_shape=jax.ShapeDtypeStruct((width, count), jnp.float32),
        scratch_shapes=[
            pltpu.VMEM((rows, LANES), jnp.float32),
            pltpu.VMEM((count, 2 * LANES), jnp.float32),
            pltpu.VMEM(idx.shape, jnp.int32),
        ] + [pltpu.VMEM((2 * total, LANES), jnp.float32)] * RING
        + [pltpu.VMEM((group * 2 * LANES, 2 * LANES), jnp.bfloat16)]
        + [pltpu.SMEM(idx.shape[1:], jnp.int32)] * RING
        + [pltpu.SemaphoreType.DMA((RING,)), pltpu.SemaphoreType.DMA] + extra,
        compiler_params=pltpu.CompilerParams(vmem_limit_bytes=56 * 2**20),
        cost_estimate=pl.CostEstimate(
            flops=2 * noff * count * 256 * 256 * 3, bytes_accessed=20 * 2**20, transcendentals=0),
    )(*operands).T


def place_cells(cells, table, base):
    count, width = cells.shape
    table[pl.ds(base, count, stride=2), :] = cells[:, 0:LANES].astype(jnp.float32)
    rest = jnp.pad(cells[:, LANES:width].astype(jnp.float32), ((0, 0), (0, 2 * LANES - width)))
    table[pl.ds(base + 1, count, stride=2), :] = rest


def pick_kernel(capacity, first, idx_ref, cells_ref, *refs):
    out_ref, table, twice, f0, f1, s0, s1, sem = refs[-8:]
    step = pl.program_id(0)
    steps = pl.num_programs(0)
    rows_f, smem = (f0, f1), (s0, s1)
    lines = s0.shape[0]
    rows, lane = capacity // SPLIT, LANES // SPLIT

    def fetch(k, s):
        return pltpu.make_async_copy(twice.at[pl.ds((2 * (first + s) + k) * lines, lines)], smem[k], sem.at[k])

    @pl.when(step == 0)
    def _():
        twice[...] = 2 * idx_ref[...]
        for k in range(2):
            fetch(k, 0).start()
        place_cells(cells_ref[...], table, 0)

    for k in range(2):
        fetch(k, step).wait()
        for r in range(lines):
            for u in range(capacity):
                rows_f[k][pl.ds(2 * (r * capacity + u), 2), :] = table[pl.ds(smem[k][r, u], 2), :]
            base = 2 * r * capacity
            out_ref[k * lines + r, 0:capacity] = rows_f[k][pl.ds(base, capacity, stride=2), :].astype(jnp.bfloat16)
            rest = rows_f[k][pl.ds(base + 1, rows, stride=2), :]
            for j in range(1, SPLIT):
                part = rows_f[k][pl.ds(base + 1 + 2 * j * rows, rows, stride=2), :]
                rest += pltpu.roll(part, j * lane, axis=1)
            out_ref[k * lines + r, capacity:] = rest.astype(jnp.bfloat16)

        @pl.when(step + 1 < steps)
        def _():
            fetch(k, step + 1).start()


def pick_rows(cells, chosen, half, partial=None):
    devices, capacity = chosen.shape
    lines = 8
    steps = devices // (4 * lines)
    first = half * steps
    operands = [chosen, cells]
    in_specs = [pl.BlockSpec(x.shape, lambda s: (0, 0), pipeline_mode=pl.Buffered(1)) for x in operands]
    if partial is not None:
        operands.append(partial)
        in_specs.append(pl.BlockSpec(memory_space=pl.ANY))
    return pl.pallas_call(
        functools.partial(pick_kernel, capacity, first),
        grid=(steps,),
        in_specs=in_specs,
        out_specs=pl.BlockSpec((2 * lines, capacity + capacity // SPLIT, LANES), lambda s: (first + s, 0, 0)),
        out_shape=jax.ShapeDtypeStruct((devices, capacity + capacity // SPLIT, LANES), jnp.bfloat16),
        scratch_shapes=[pltpu.VMEM((2 * cells.shape[0], LANES), jnp.float32), pltpu.VMEM(chosen.shape, jnp.int32)]
        + [pltpu.VMEM((2 * lines * capacity, LANES), jnp.float32)] * 2
        + [pltpu.SMEM((lines, capacity), jnp.int32)] * 2
        + [pltpu.SemaphoreType.DMA((2,))],
        input_output_aliases={} if partial is None else {2: 0},
        compiler_params=pltpu.CompilerParams(vmem_limit_bytes=56 * 2**20),
        cost_estimate=pl.CostEstimate(flops=0, bytes_accessed=24 * 2**20, transcendentals=0),
    )(*operands)


def two_rows(x):
    return jnp.pad(x, ((0, 0), (0, 2 * LANES - x.shape[1]))).reshape(2 * x.shape[0], LANES)


def lines_of(index):
    used = index.shape[1]
    lines = -(-used // LANES)
    return jnp.pad(index, ((0, 0), (0, lines * LANES - used))).reshape(index.shape[0], lines, LANES)


def local(leaf_density, m2l_matrices, m2m_matrices, send_index, leaf_source, coarse_source):
    cells, width = leaf_density.shape
    noff = m2l_matrices.shape[0]
    parents_here = cells // 8
    narrow = lax.axis_size("narrow")
    wide = lax.axis_size("wide")
    parents = jnp.dot(
        leaf_density.reshape(parents_here, 8 * width),
        m2m_matrices.reshape(8 * width, width),
        preferred_element_type=jnp.float32,
    ).astype(jnp.bfloat16)
    own = two_rows(parents)
    group = lax.all_to_all(
        jnp.broadcast_to(own, (narrow,) + own.shape), "narrow", split_axis=0, concat_axis=0, tiled=True
    ).reshape(narrow * own.shape[0], LANES)

    chosen = send_index[0]
    outgoing = pick_rows(leaf_density, chosen, 0)
    outgoing, group = lax.optimization_barrier((outgoing, group))
    up = [(i, i + 1) for i in range(wide - 1)]
    down = [(j, i) for i, j in up]
    before = lax.ppermute(group, "wide", up)
    after = lax.ppermute(group, "wide", down)
    outgoing = pick_rows(leaf_density, chosen, 1, outgoing)
    outgoing, before, after, m2l_matrices, leaf_source, coarse_source = lax.optimization_barrier(
        (outgoing, before, after, m2l_matrices, leaf_source, coarse_source)
    )
    far = lax.all_to_all(outgoing, ("wide", "narrow"), split_axis=0, concat_axis=0, tiled=True)

    near = jnp.concatenate([before, group, after], axis=0)
    base = (lax.axis_index("wide") - 1) * (narrow * parents_here)
    coarse_row = jnp.where(coarse_source < 0, 0, ZERO + 2 * (coarse_source - base))
    together = 9
    coarse_index = lines_of(coarse_row.reshape(noff // together, together * parents_here))
    coarse_local = translate(coarse_index, m2l_matrices, near, None, together, parents_here, 0.5, 3, 1)

    leaf_index = lines_of(
        jnp.where(leaf_source < 0, 0, ZERO + 2 * leaf_source).reshape(noff // LEAF_GROUP, LEAF_GROUP * cells)
    )
    far, leaf_index, coarse_local = lax.optimization_barrier((far, leaf_index, coarse_local))
    leaf_local = translate(leaf_index, m2l_matrices, leaf_density, far, LEAF_GROUP, cells, 1, LEAF_BURST, LEAF_PIECES)
    return (leaf_local, parents, coarse_local)


def solution(mesh):
    rows = P(("wide", "narrow"), None)
    columns = P(None, ("wide", "narrow"))
    return jax.shard_map(
        local,
        mesh=mesh,
        in_specs=(rows, P(), P(), P(("wide", "narrow"), None, None), columns, columns),
        out_specs=(rows, rows, rows),
        check_vma=False,
    )
```

```python
import functools

import jax
import jax.numpy as jnp
from jax import lax
from jax.experimental import pallas as pl
from jax.experimental.pallas import tpu as pltpu
from jax.sharding import PartitionSpec as P

LANES = 128
SPLIT = 4
RING = 3
ZERO = 8
PARTS = 4
LEAF_GROUP = 1
LEAF_BURST = 9
LEAF_PIECES = 2


def place_far(block, table, base):
    count = block.shape[0] * SPLIT // (SPLIT + 1)
    rows, step = count // SPLIT, LANES // SPLIT
    table[pl.ds(base, count, stride=2), :] = block[0:count].astype(jnp.float32)
    rest = block[count:].astype(jnp.float32)
    for j in range(SPLIT):
        part = rest if j == 0 else pltpu.roll(rest, LANES - j * step, axis=1)
        table[pl.ds(base + 1 + 2 * j * rows, rows, stride=2), :] = part


def translate_kernel(group, count, scale, packed, burst, pieces, idx_hbm, m2l_ref, *refs):
    near_ref, refs = refs[0], refs[1:]
    if packed:
        far_hbm, refs = refs[0:2], refs[2:]
    out_ref, table, acc, idx_vmem = refs[:4]
    rows_f, kept, smem = refs[4:7], refs[7], refs[8:11]
    sem, vsem = refs[11:13]
    step = pl.program_id(0)
    steps = pl.num_programs(0)
    width = m2l_ref.shape[1]
    total = group * count

    def fetch(k, c):
        return pltpu.make_async_copy(idx_vmem.at[c], smem[k], sem.at[k])

    def gather(k, lo, hi):
        for t in range(lo, hi):
            i = smem[k][t // LANES, t % LANES]
            rows_f[k][pl.ds(2 * t, 2), :] = table[pl.ds(i, 2), :]

    def multiply(k, lo, hi, matrix):
        sides = []
        for g in range(group):
            for side in range(2):
                rows = pl.ds(2 * (g * count + lo) + side, hi - lo, stride=2)
                sides.append(rows_f[k][rows, :].astype(jnp.bfloat16))
        acc[lo:hi] += jnp.dot(jnp.concatenate(sides, axis=1), matrix, preferred_element_type=jnp.float32)

    def matrix_of(c):
        room = 2 * LANES - width
        return jnp.concatenate([jnp.pad(m2l_ref[c * group + g], ((0, room), (0, room))) for g in range(group)], axis=0)

    @pl.when(step == 0)
    def _():
        copy = pltpu.make_async_copy(idx_hbm, idx_vmem, vsem)
        copy.start()
        if packed:
            far, fsem = refs[13:15], refs[15]
            span = far[0].shape[0] // PARTS
            slots = far[0].shape[1] * SPLIT // (SPLIT + 1)

            def part(h, q):
                place = pl.ds(q * span, span)
                return pltpu.make_async_copy(far_hbm[h].at[place], far[h].at[place], fsem.at[h, q])

            for h in range(2):
                for q in range(PARTS):
                    part(h, q).start()
        acc[...] = jnp.zeros_like(acc)
        last = rows_f[(burst - 1) % RING]
        last[...] = jnp.zeros_like(last)
        kept[...] = jnp.zeros_like(kept)
        table[0:ZERO, :] = jnp.zeros((ZERO, LANES), jnp.float32)
        copy.wait()
        for k in range(RING):
            fetch(k, k).start()
        n = near_ref.shape[0]
        if packed:
            place_cells(near_ref[...], table, ZERO)
            n = 2 * n
        else:
            table[pl.ds(ZERO, n), :] = near_ref[...].astype(jnp.float32)
        if packed:
            for h in range(2):
                for q in range(PARTS):
                    part(h, q).wait()

                    @pl.loop(0, span)
                    def _(b):
                        p = q * span + b
                        base = ZERO + n + p * 4 * slots + h * 2 * slots
                        place_far(far[h][p], table, pl.multiple_of(base, 8))

    for c in range(burst):
        k = c % RING
        fetch(k, burst * step + c).wait()
        matrix = kept[...] if c == 0 else matrix_of(c - 1)
        for p in range(pieces):
            gather(k, total * p // pieces, total * (p + 1) // pieces)
            multiply((c + burst - 1) % burst % RING, count * p // pieces, count * (p + 1) // pieces, matrix)

        @pl.when(burst * step + c + RING < burst * steps)
        def _():
            fetch(k, burst * step + c + RING).start()

    kept[...] = matrix_of(burst - 1)

    @pl.when(step == steps - 1)
    def _():
        multiply((burst - 1) % RING, 0, count, kept[...])
        total_t = acc[...].T[0:width]
        out_ref[...] = scale * total_t if scale != 1 else total_t


def translate(idx, m2l, near2, far, group, count, scale, burst, pieces):
    noff, width, _ = m2l.shape
    rows = ZERO + near2.shape[0] * (1 if far is None else 2)
    total = group * count
    operands = [idx, m2l, near2]
    in_specs = [
        pl.BlockSpec(memory_space=pl.ANY),
        pl.BlockSpec((burst * group, width, width), lambda s: (s, 0, 0)),
        pl.BlockSpec(near2.shape, lambda s: (0, 0), pipeline_mode=pl.Buffered(1)),
    ]
    extra = []
    if far is not None:
        rows += 4 * far[0].shape[0] * far[0].shape[1] * SPLIT // (SPLIT + 1)
        operands += far
        in_specs += [pl.BlockSpec(memory_space=pl.ANY)] * 2
        extra = [pltpu.VMEM(x.shape, x.dtype) for x in far] + [pltpu.SemaphoreType.DMA((2, PARTS))]
    return pl.pallas_call(
        functools.partial(translate_kernel, group, count, scale, far is not None, burst, pieces),
        grid=(noff // (burst * group),),
        in_specs=in_specs,
        out_specs=pl.BlockSpec((width, count), lambda s: (0, 0)),
        out_shape=jax.ShapeDtypeStruct((width, count), jnp.float32),
        scratch_shapes=[
            pltpu.VMEM((rows, LANES), jnp.float32),
            pltpu.VMEM((count, 2 * LANES), jnp.float32),
            pltpu.VMEM(idx.shape, jnp.int32),
        ] + [pltpu.VMEM((2 * total, LANES), jnp.float32)] * RING
        + [pltpu.VMEM((group * 2 * LANES, 2 * LANES), jnp.bfloat16)]
        + [pltpu.SMEM(idx.shape[1:], jnp.int32)] * RING
        + [pltpu.SemaphoreType.DMA((RING,)), pltpu.SemaphoreType.DMA] + extra,
        compiler_params=pltpu.CompilerParams(vmem_limit_bytes=56 * 2**20),
        cost_estimate=pl.CostEstimate(
            flops=2 * noff * count * 256 * 256 * 3, bytes_accessed=20 * 2**20, transcendentals=0),
    )(*operands).T


def place_cells(cells, table, base):
    count, width = cells.shape
    table[pl.ds(base, count, stride=2), :] = cells[:, 0:LANES].astype(jnp.float32)
    rest = jnp.pad(cells[:, LANES:width].astype(jnp.float32), ((0, 0), (0, 2 * LANES - width)))
    table[pl.ds(base + 1, count, stride=2), :] = rest


def pick_kernel(capacity, first, idx_ref, cells_ref, out_ref, table, twice, f0, f1, s0, s1, sem):
    step = pl.program_id(0)
    steps = pl.num_programs(0)
    rows_f, smem = (f0, f1), (s0, s1)
    lines = s0.shape[0]
    rows, lane = capacity // SPLIT, LANES // SPLIT

    def fetch(k, s):
        return pltpu.make_async_copy(twice.at[pl.ds((2 * s + k) * lines, lines)], smem[k], sem.at[k])

    @pl.when(step == 0)
    def _():
        twice[...] = 2 * idx_ref[:, first:first + capacity]
        for k in range(2):
            fetch(k, 0).start()
        place_cells(cells_ref[...], table, 0)

    for k in range(2):
        fetch(k, step).wait()
        for r in range(lines):
            for u in range(capacity):
                rows_f[k][pl.ds(2 * (r * capacity + u), 2), :] = table[pl.ds(smem[k][r, u], 2), :]
            base = 2 * r * capacity
            out_ref[k * lines + r, 0:capacity] = rows_f[k][pl.ds(base, capacity, stride=2), :].astype(jnp.bfloat16)
            rest = rows_f[k][pl.ds(base + 1, rows, stride=2), :]
            for j in range(1, SPLIT):
                part = rows_f[k][pl.ds(base + 1 + 2 * j * rows, rows, stride=2), :]
                rest += pltpu.roll(part, j * lane, axis=1)
            out_ref[k * lines + r, capacity:] = rest.astype(jnp.bfloat16)

        @pl.when(step + 1 < steps)
        def _():
            fetch(k, step + 1).start()


def pick_rows(cells, chosen, half):
    devices, capacity = chosen.shape[0], chosen.shape[1] // 2
    lines = 16
    operands = [chosen, cells]
    return pl.pallas_call(
        functools.partial(pick_kernel, capacity, half * capacity),
        grid=(devices // (2 * lines),),
        in_specs=[pl.BlockSpec(x.shape, lambda s: (0, 0), pipeline_mode=pl.Buffered(1)) for x in operands],
        out_specs=pl.BlockSpec((2 * lines, capacity + capacity // SPLIT, LANES), lambda s: (s, 0, 0)),
        out_shape=jax.ShapeDtypeStruct((devices, capacity + capacity // SPLIT, LANES), jnp.bfloat16),
        scratch_shapes=[pltpu.VMEM((2 * cells.shape[0], LANES), jnp.float32), pltpu.VMEM((devices, capacity), jnp.int32)]
        + [pltpu.VMEM((2 * lines * capacity, LANES), jnp.float32)] * 2
        + [pltpu.SMEM((lines, capacity), jnp.int32)] * 2
        + [pltpu.SemaphoreType.DMA((2,))],
        compiler_params=pltpu.CompilerParams(vmem_limit_bytes=56 * 2**20),
        cost_estimate=pl.CostEstimate(flops=0, bytes_accessed=24 * 2**20, transcendentals=0),
    )(*operands)


def two_rows(x):
    return jnp.pad(x, ((0, 0), (0, 2 * LANES - x.shape[1]))).reshape(2 * x.shape[0], LANES)


def lines_of(index):
    used = index.shape[1]
    lines = -(-used // LANES)
    return jnp.pad(index, ((0, 0), (0, lines * LANES - used))).reshape(index.shape[0], lines, LANES)


def local(leaf_density, m2l_matrices, m2m_matrices, send_index, leaf_source, coarse_source):
    cells, width = leaf_density.shape
    noff = m2l_matrices.shape[0]
    parents_here = cells // 8
    narrow = lax.axis_size("narrow")
    wide = lax.axis_size("wide")
    parents = jnp.dot(
        leaf_density.reshape(parents_here, 8 * width),
        m2m_matrices.reshape(8 * width, width),
        preferred_element_type=jnp.float32,
    ).astype(jnp.bfloat16)
    own = two_rows(parents)
    group = lax.all_to_all(
        jnp.broadcast_to(own, (narrow,) + own.shape), "narrow", split_axis=0, concat_axis=0, tiled=True
    ).reshape(narrow * own.shape[0], LANES)

    chosen = send_index[0]
    one = pick_rows(leaf_density, chosen, 0)
    one, group = lax.optimization_barrier((one, group))
    up = [(i, i + 1) for i in range(wide - 1)]
    down = [(j, i) for i, j in up]
    before = lax.ppermute(group, "wide", up)
    after = lax.ppermute(group, "wide", down)
    one, before, after, leaf_later = lax.optimization_barrier((one, before, after, leaf_density))
    far_one = lax.all_to_all(one, ("wide", "narrow"), split_axis=0, concat_axis=0, tiled=True)
    two = pick_rows(leaf_later, chosen, 1)
    two, m2l_matrices, leaf_source, coarse_source = lax.optimization_barrier(
        (two, m2l_matrices, leaf_source, coarse_source)
    )
    far_two = lax.all_to_all(two, ("wide", "narrow"), split_axis=0, concat_axis=0, tiled=True)

    near = jnp.concatenate([before, group, after], axis=0)
    base = (lax.axis_index("wide") - 1) * (narrow * parents_here)
    coarse_row = jnp.where(coarse_source < 0, 0, ZERO + 2 * (coarse_source - base))
    together = 9
    coarse_index = lines_of(coarse_row.reshape(noff // together, together * parents_here))
    coarse_local = translate(coarse_index, m2l_matrices, near, None, together, parents_here, 0.5, 3, 1)

    leaf_index = lines_of(
        jnp.where(leaf_source < 0, 0, ZERO + 2 * leaf_source).reshape(noff // LEAF_GROUP, LEAF_GROUP * cells)
    )
    far_one, far_two, leaf_index, coarse_local = lax.optimization_barrier((far_one, far_two, leaf_index, coarse_local))
    leaf_local = translate(leaf_index, m2l_matrices, leaf_density, [far_one, far_two], LEAF_GROUP, cells, 1, LEAF_BURST, LEAF_PIECES)
    return (leaf_local, parents, coarse_local)


def solution(mesh):
    rows = P(("wide", "narrow"), None)
    columns = P(None, ("wide", "narrow"))
    return jax.shard_map(
        local,
        mesh=mesh,
        in_specs=(rows, P(), P(), P(("wide", "narrow"), None, None), columns, columns),
        out_specs=(rows, rows, rows),
        check_vma=False,
    )
```
